32 devices in a mesh: section: 2 (over x), expert: 16 (over z, y, core).
Axes of the slice: x: 2, y: 2, z: 4, core: 2. Of those that a mesh axis runs over, the one named last changes fastest.
Arguments:
- histories: bfloat16 [2, 2048, 5120], P('section', 'expert'), may hold values from -6 to 6
- page_map: int32 [2, 2, 512], P('section', None, 'expert'), may hold values from 0 to 511, as said below
- user_pages: int32 [2, 16, 4], P('section', 'expert'), may hold values from 1 to 16, 32 in all within a row
- tails: int32 [2, 16, 4], P('section', 'expert'), may hold values from 1 to 4
- routes: int32 [2, 2048, 2], P('section', 'expert'), may hold values from 0 to 7, all different within a row; in each aligned block of 128 rows (0 to 127, 128 to 255, ..., all dimensions but the last counted through in order) at most 64 rows name the same one
- out_proj: bfloat16 [2, 1024, 1024], P('section', 'expert'), may hold values from -0.1875 to 0.1875
- router: bfloat16 [2, 1024, 8], P('section'), may hold values from -0.75 to 0.75
- w_gate: bfloat16 [2, 1024, 8192], P('section', None, 'expert'), may hold values from -0.1875 to 0.1875
- w_up: bfloat16 [2, 1024, 8192], P('section', None, 'expert'), may hold values from -0.1875 to 0.1875
- w_down: bfloat16 [2, 8192, 1024], P('section', 'expert'), may hold values from -0.1875 to 0.1875
Outputs:
- handed: bfloat16 [2, 2048, 1024], P('section', 'expert')
The draws below stay inside these ranges and needn't reach their ends.
Inputs may be any that keep to these rules, and one draw needn't show every extreme that they name: page_map[0] is a permutation of the pages of a section and page_map[1] its inverse; every device holds exactly 32 pages before and after; no device's pages send more than 2 pages to one device, and some send exactly 2. `user_pages`: the 4 entries of one device sum to 32, and the largest is 16. `routes`: A row names 2 different experts; among the rows of one device, no expert is named more than 64 times, a bound that some block reaches.
All inputs are finite; a program needn't handle non-finite values.
Results may differ from the reference program's by a relative error of at most 0.012.
Values may be sent and summed in bfloat16 or wider, within the bound.
A program may use at most 64 MiB of HBM per device.

```python
import math
import jax
import jax.numpy as jnp
import numpy as np
from jax import lax

D = 1024
HEADS = 8
HID = 1024
EXPERTS = 8
TOP = 2
PAGE = 4
PAGES_DEV = 32
USERS_DEV = 4
MAXPAGES = 16
TOK_DEV = 128
TOKENS = 2048
NPAGES = 512
SECTIONS = 2
CAP = 64
N_EXPERT = 16


def section_pages(section_key):
    device_count = N_EXPERT
    first_key, second_key, third_key, fourth_key, fifth_key = jax.random.split(section_key, 5)
    place_perm = jax.random.permutation(first_key, device_count).astype(jnp.int32)
    shift_perm = jax.random.permutation(second_key, device_count).astype(jnp.int32)
    offset_perm = jax.random.permutation(third_key, device_count).astype(jnp.int32)
    page_index = jnp.arange(PAGES_DEV, dtype=jnp.int32)
    offsets = offset_perm[page_index % device_count]
    sender = jnp.arange(device_count, dtype=jnp.int32)
    receiver = place_perm[(shift_perm[:, None] + offsets[None, :]) % device_count]
    arrival_perm = jax.vmap(lambda sub_key: jax.random.permutation(sub_key, PAGES_DEV))(jax.random.split(fourth_key, device_count)).astype(jnp.int32)
    holding_perm = jax.vmap(lambda sub_key: jax.random.permutation(sub_key, PAGES_DEV))(jax.random.split(fifth_key, device_count)).astype(jnp.int32)
    arrival_slot = arrival_perm[receiver, page_index[None, :]]
    global_target = (receiver * PAGES_DEV + arrival_slot).reshape(-1).astype(jnp.int32)
    global_source = (sender[:, None] * PAGES_DEV + holding_perm).reshape(-1).astype(jnp.int32)
    forward = jnp.zeros((NPAGES,), jnp.int32).at[global_source].set(global_target)
    inverse = jnp.zeros((NPAGES,), jnp.int32).at[global_target].set(global_source)
    return jnp.stack([forward, inverse])


def draw_page_map(key, part):
    return jax.vmap(section_pages)(jax.random.split(jax.random.fold_in(key, 11), SECTIONS))


def plant(entries, stream_key, low, high):
    place = [jax.random.randint(jax.random.fold_in(stream_key, axis), (), 0, length) for axis, length in enumerate(entries.shape)]
    main_axis = entries.shape.index(max(entries.shape))
    next_to = place[:main_axis] + [(place[main_axis] + 1) % entries.shape[main_axis]] + place[main_axis + 1:]
    return entries.at[tuple(place)].set(low).at[tuple(next_to)].set(high)


def levels(key, extent, shards, least, largest):
    loudness, own = 1.0, jax.random.fold_in(key, 6)
    for axis_at, shards_of in shards:
        draws = jnp.exp(jax.random.uniform(jax.random.fold_in(own, axis_at), (shards_of,), jnp.float32, least / len(shards), largest / len(shards)))
        loudness = loudness * jnp.repeat(draws, extent[axis_at] // shards_of).reshape([-1 if axis == axis_at else 1 for axis in range(len(extent))])
    return loudness


def length_profile(amount, total, most, slope):
    weights = [(1 << 20) // math.isqrt(standing ** slope) + 1 for standing in range(2, amount + 1)]
    spare, given = total - most - (amount - 1), [1] * (amount - 1)
    while spare > 0:
        movable = [i for i in range(amount - 1) if given[i] < most]
        mass, remaining = sum([weights[i] for i in movable]), spare
        for i in movable:
            addition = min(most - given[i], max(1, remaining * weights[i] // mass), spare)
            given[i] = given[i] + addition
            spare = spare - addition
    return np.array([most] + given)


def ragged_sizes(rng, number_of, total, bound, lean):
    if number_of == 2:
        one = jax.random.randint(rng, (), max(1, total - bound), min(bound, total - 1) + 1)
        return jnp.stack([one, total - one])
    lengths = jnp.asarray(length_profile(number_of, total, bound, lean), jnp.int32)
    twos = (number_of - 1) // 2
    source_of, taker = lengths[1:1 + 2 * twos:2], lengths[2:2 + 2 * twos:2]
    margin = jnp.minimum(source_of - 1, bound - taker)
    moved = jax.random.randint(jax.random.fold_in(rng, 1), (twos,), 0, 1 << 20) % (margin + 1)
    lengths = lengths.at[1:1 + 2 * twos:2].set(source_of - moved).at[2:2 + 2 * twos:2].set(taker + moved)
    return lengths[jax.random.permutation(jax.random.fold_in(rng, 2), number_of)]


def shared_out(key, own, number, rows, number_of, top, most, skew):
    order = jax.random.permutation(key, number_of)
    heavy_load, ordinary = load_shares(number_of, rows * top, most, skew, True), load_shares(number_of, rows * top, most, skew, False)
    places = jnp.arange(number_of)

    def named(sizes, turn):
        used = int((sizes > 0).sum())
        fixed = max(1, used // 4)
        passed = fixed + (places - fixed + turn * (used - fixed)) % max(1, number_of - fixed)
        return jnp.zeros((number_of,), jnp.int32).at[order[jnp.where(places < fixed, places, passed)]].set(jnp.asarray(sizes, jnp.int32))

    sizes = jnp.where(number % 4 == 0, named(heavy_load, number // 4), named(ordinary, number - number // 4 - 1))
    mixed = jax.random.permutation(jax.random.fold_in(own, 3), number_of)
    donor, taker = mixed[0:number_of // 2 * 2:2], mixed[1:number_of // 2 * 2:2]
    room = jnp.minimum(sizes[donor] - 1, most - sizes[taker]) // 2
    room = jnp.where((donor == order[0]) | (taker == order[0]) | (sizes[taker] == 0), 0, jnp.maximum(room, 0))
    passed = jax.random.randint(jax.random.fold_in(own, 4), (number_of // 2,), 0, 1 << 20) % (room + 1)
    sizes = sizes.at[donor].add(-passed).at[taker].add(passed)
    items = jnp.searchsorted(jnp.cumsum(sizes), jnp.arange(rows * top), side="right").astype(jnp.int32)
    grid = items.reshape(top, rows).T
    grid = grid[jax.random.permutation(jax.random.fold_in(own, 1), rows)]
    turn = jax.random.randint(jax.random.fold_in(own, 2), (rows, 1), 0, top)
    return jnp.take_along_axis(grid, (jnp.arange(top)[None, :] + turn) % top, axis=1)


def load_shares(amount, total, limit, slope, full):
    portions = [(1 << 20) // math.isqrt(standing ** slope) + 1 for standing in range(1, amount + 1)]
    largest = limit if full else min(limit, max(-(-total // amount), total * portions[0] // sum(portions)))
    least = 1 if total - largest >= amount - 1 else 0
    holding, rest = [largest] + [least] * (amount - 1), total - largest - least * (amount - 1)
    while rest > 0:
        free = [i for i in range(1, amount) if holding[i] < largest] or [i for i in range(1, amount) if holding[i] < limit]
        whole, remaining = sum([portions[i] for i in free]), rest
        for i in free:
            extra = min(limit - holding[i], max(1, remaining * portions[i] // whole), rest)
            holding[i] = holding[i] + extra
            rest = rest - extra
    return np.array(holding)


def normal_values(own_key, extent, scale, limit, pieces=(), held_as=jnp.bfloat16):
    level = levels(own_key, extent, pieces, -0.22, 0.18) if pieces else 1.0
    values = jax.random.normal(own_key, extent, jnp.float32) * scale * level
    return jnp.minimum(jnp.maximum(values, -limit), limit).astype(held_as)


def setup_inputs(seed: int = 0) -> dict:
    streams_of = jax.random.split(jax.random.key(seed), 11)
    histories = normal_values(streams_of[0], (SECTIONS, TOKENS, 5 * D), 1.0, 6.0, ((0, 2), (1, 16)))
    page_map = draw_page_map(jax.random.fold_in(streams_of[10], 71), 0)
    user_pages = jax.vmap(lambda own: ragged_sizes(own, USERS_DEV, PAGES_DEV, MAXPAGES, 2))(jax.random.split(streams_of[2], SECTIONS * N_EXPERT)).reshape((SECTIONS, N_EXPERT, USERS_DEV)).astype(jnp.int32)
    tails = plant(jax.random.randint(streams_of[3], (SECTIONS, N_EXPERT, USERS_DEV), 1, PAGE + 1), jax.random.fold_in(streams_of[3], 1), 1, PAGE).astype(jnp.int32)
    routes_keys = jax.random.split(jax.random.fold_in(streams_of[4], 1), SECTIONS * TOKENS // TOK_DEV)
    routes_turns = jax.random.permutation(jax.random.fold_in(streams_of[4], 3), SECTIONS * TOKENS // TOK_DEV)
    routes = jax.vmap(lambda own, number: shared_out(jax.random.fold_in(streams_of[4], 2), own, number, TOK_DEV, EXPERTS, TOP, CAP, 2))(routes_keys, routes_turns).reshape((SECTIONS, TOKENS, TOP))
    out_proj = normal_values(streams_of[5], (SECTIONS, D, D), D ** -0.5, 0.1875, ((0, 2), (1, 16)))
    router = normal_values(streams_of[6], (SECTIONS, D, EXPERTS), (D // 16) ** -0.5, 0.75, ((0, 2),))
    w_gate = normal_values(streams_of[7], (SECTIONS, D, EXPERTS * HID), D ** -0.5, 0.1875, ((0, 2), (2, 16)))
    w_up = normal_values(streams_of[8], (SECTIONS, D, EXPERTS * HID), D ** -0.5, 0.1875, ((0, 2), (2, 16)))
    w_down = normal_values(streams_of[9], (SECTIONS, EXPERTS * HID, D), HID ** -0.5, 0.1875, ((0, 2), (1, 16)))
    return dict(histories=histories, page_map=page_map, user_pages=user_pages, tails=tails, routes=routes, out_proj=out_proj, router=router, w_gate=w_gate, w_up=w_up, w_down=w_down)


def layout_rows(counts, tail_rows, page_rows, row_count):
    counts = counts.astype(jnp.int32)
    starting = (jnp.cumsum(counts) - counts).astype(jnp.int32)
    length = ((counts - 1) * page_rows + tail_rows).astype(jnp.int32)
    row_index = jnp.arange(row_count, dtype=jnp.int32)
    page_of = row_index // page_rows
    owner_of = lax.optimization_barrier(jnp.sum((starting[None, :] <= page_of[:, None]).astype(jnp.int32), axis=1)) - 1
    member = owner_of[:, None] == jnp.arange(counts.shape[0], dtype=jnp.int32)[None, :]
    offset = lax.optimization_barrier(jnp.sum(jnp.where(member, starting[None, :] * page_rows, 0), axis=1))
    spread = lax.optimization_barrier(jnp.sum(jnp.where(member, length[None, :], 0), axis=1))
    return (owner_of, row_index - offset, spread)

def attend(balanced, counts, tail_rows):
    row_count = balanced.shape[0]
    model_width = balanced.shape[1] // 5
    head_dim = model_width // HEADS
    owner_of, position, spread = layout_rows(counts, tail_rows, PAGE, row_count)
    allowed = (owner_of[:, None] == owner_of[None, :]) & (position[None, :] <= position[:, None]) & (position[None, :] < spread[None, :])
    queries = balanced[:, :model_width].reshape(row_count, HEADS, head_dim).astype(jnp.float32)
    key_rows = balanced[:, model_width:2 * model_width].reshape(row_count, HEADS, head_dim).astype(jnp.float32)
    values = balanced[:, 2 * model_width:3 * model_width].reshape(row_count, HEADS, head_dim)
    scores = jnp.einsum('qhd,khd->hqk', queries, key_rows) * head_dim ** (-0.5)
    weights = jnp.where(allowed[None], jax.nn.silu(scores), 0.0) / spread.astype(jnp.float32)[None, :, None]
    weights = weights.astype(jnp.bfloat16)
    attended = jnp.einsum('hqk,khd->qhd', weights.astype(jnp.float32), values.astype(jnp.float32)).reshape(row_count, model_width)
    average = lax.optimization_barrier(jnp.mean(attended, axis=1, keepdims=True))
    centered = attended - average
    variance = lax.optimization_barrier(jnp.mean(centered * centered, axis=1, keepdims=True))
    gating = balanced[:, 3 * model_width:4 * model_width].astype(jnp.float32)
    return (centered * lax.rsqrt(variance + 1e-05) * gating).astype(jnp.bfloat16)

def gate_share(normed, router, routes):
    logits = jnp.dot(normed, router, preferred_element_type=jnp.float32)
    scores = jax.nn.sigmoid(logits)
    picked = routes[:, :, None] == jnp.arange(router.shape[1], dtype=jnp.int32)[None, None, :]
    chosen = lax.optimization_barrier(jnp.sum(jnp.where(picked, scores[:, None, :], 0.0), axis=2))
    return chosen / lax.optimization_barrier(jnp.sum(chosen, axis=1, keepdims=True))

def slot_table(routes, experts, capacity):
    pair_count = routes.shape[0] * routes.shape[1]
    chosen = routes.reshape(-1).astype(jnp.int32)
    onehot = (chosen[:, None] == jnp.arange(experts, dtype=jnp.int32)[None, :]).astype(jnp.int32)
    before = jnp.cumsum(onehot, axis=0) - onehot
    ranking = lax.optimization_barrier(jnp.sum(before * onehot, axis=1)).astype(jnp.int32)
    slot_of_pair = chosen * capacity + ranking
    matches = slot_of_pair[None, :] == jnp.arange(experts * capacity, dtype=jnp.int32)[:, None]
    source_token = lax.optimization_barrier(jnp.sum(jnp.where(matches, jnp.arange(pair_count, dtype=jnp.int32)[None, :], 0), axis=1)) // 2
    return (slot_of_pair, source_token.astype(jnp.int32))

def expert_ffn(flat_rows, gate_cols, up_cols, down_rows):
    gate_act = jnp.dot(flat_rows, gate_cols, preferred_element_type=jnp.float32)
    up_act = jnp.dot(flat_rows, up_cols, preferred_element_type=jnp.float32)
    hidden = (jax.nn.silu(gate_act) * up_act).astype(jnp.bfloat16)
    half_units = HID // 2
    first_part = jnp.dot(hidden[:, :half_units], down_rows[:half_units], preferred_element_type=jnp.float32).astype(jnp.bfloat16)
    second_part = jnp.dot(hidden[:, half_units:], down_rows[half_units:], preferred_element_type=jnp.float32).astype(jnp.bfloat16)
    return (first_part.astype(jnp.float32) + second_part.astype(jnp.float32)).astype(jnp.bfloat16)

def one_section(histories, page_map, user_pages, tails, routes, out_proj, router, w_gate, w_up, w_down):
    page_block = histories.reshape(NPAGES, PAGE, 5 * D)
    placed = jnp.zeros_like(page_block).at[page_map[0].astype(jnp.int32)].set(page_block)
    balanced = placed.reshape(N_EXPERT, TOK_DEV, 5 * D)
    mixed_in = lax.map(lambda item_pack: attend(item_pack[0], item_pack[1], item_pack[2]), (balanced, user_pages, tails))
    mixed_in = mixed_in.reshape(TOKENS, D)
    flat_rows = balanced.reshape(TOKENS, 5 * D)
    resid = (flat_rows[:, 4 * D:].astype(jnp.float32) + jnp.dot(mixed_in, out_proj, preferred_element_type=jnp.float32)).astype(jnp.bfloat16)
    resid_wide = resid.astype(jnp.float32)
    normed = (resid_wide * lax.rsqrt(lax.optimization_barrier(jnp.mean(resid_wide * resid_wide, axis=1, keepdims=True)) + 1e-06)).astype(jnp.bfloat16)
    share = gate_share(normed, router, routes)
    slot_of_pair, source_token = jax.vmap(lambda group: slot_table(group, EXPERTS, CAP))(routes.reshape(N_EXPERT, TOK_DEV, 2))
    token_ids = source_token + (jnp.arange(N_EXPERT, dtype=jnp.int32) * TOK_DEV)[:, None]
    table = token_ids.reshape(N_EXPERT, EXPERTS, CAP).transpose(1, 0, 2).reshape(EXPERTS, N_EXPERT * CAP)
    gate_all = w_gate.reshape(D, EXPERTS, HID).transpose(1, 0, 2)
    up_all = w_up.reshape(D, EXPERTS, HID).transpose(1, 0, 2)
    down_all = w_down.reshape(EXPERTS, HID, D)
    outputs = lax.map(lambda item_pack: expert_ffn(normed[item_pack[0]], item_pack[1], item_pack[2], item_pack[3]), (table, gate_all, up_all, down_all))
    outputs = outputs.reshape(EXPERTS, N_EXPERT, CAP, D).transpose(1, 0, 2, 3).reshape(N_EXPERT, EXPERTS * CAP, D)
    picked = jax.vmap(lambda block_out, block_slot: block_out[block_slot])(outputs, slot_of_pair)
    picked = picked.reshape(TOKENS, 2, D).astype(jnp.float32)
    mixture = lax.optimization_barrier(jnp.sum(picked * share[:, :, None], axis=1))
    return (resid_wide + mixture).astype(jnp.bfloat16)

def reference(histories, page_map, user_pages, tails, routes, out_proj, router, w_gate, w_up, w_down):
    results = []
    for section_index in range(SECTIONS):
        results.append(one_section(histories[section_index], page_map[section_index], user_pages[section_index], tails[section_index], routes[section_index], out_proj[section_index], router[section_index], w_gate[section_index], w_up[section_index], w_down[section_index]))
    output_rows = jnp.stack(results)
    return jnp.roll(output_rows, 1, axis=0)
```

```python
import jax
import jax.numpy as jnp
from jax import lax
from jax.sharding import PartitionSpec as P

HEADS = 8


def swapped(shard, axis, apart):
    return lax.ppermute(shard, axis, [(i, i ^ 1 << apart) for i in range(lax.axis_size(axis))])


def from_behind(block, axis, distance):
    devices = range(lax.axis_size(axis))
    route = [((i - distance) % len(devices), i) for i in devices]
    return lax.ppermute(block, axis, route)


def layout_rows(counts, tail_rows, page_rows, row_count):
    member_index = jnp.arange(counts.shape[0], dtype=jnp.int32)
    ahead = member_index[None, :] < member_index[:, None]
    starting = jnp.sum(jnp.where(ahead, counts[None, :], 0), axis=1)
    length = (counts - 1) * page_rows + tail_rows
    row_index = jnp.arange(row_count, dtype=jnp.int32)
    page_of = row_index // page_rows
    owner_of = jnp.sum((starting[None, :] <= page_of[:, None]).astype(jnp.int32), axis=1) - 1
    member = owner_of[:, None] == jnp.arange(counts.shape[0], dtype=jnp.int32)[None, :]
    offset = jnp.sum(jnp.where(member, starting[None, :] * page_rows, 0), axis=1)
    spread = jnp.sum(jnp.where(member, length[None, :], 0), axis=1)
    return (owner_of, row_index - offset, spread)


def attend(balanced, counts, tail_rows, page_rows):
    row_count = balanced.shape[0]
    model_width = balanced.shape[1] // 5
    head_dim = model_width // HEADS
    owner_of, position, spread = layout_rows(counts, tail_rows, page_rows, row_count)
    allowed = (
        (owner_of[:, None] == owner_of[None, :])
        & (position[None, :] <= position[:, None])
        & (position[None, :] < spread[None, :])
    )
    queries = balanced[:, :model_width].reshape(row_count, HEADS, head_dim)
    key_rows = balanced[:, model_width : 2 * model_width].reshape(row_count, HEADS, head_dim)
    values = balanced[:, 2 * model_width : 3 * model_width].reshape(row_count, HEADS, head_dim)
    scores = jnp.einsum(
        "qhd,khd->hqk", queries, key_rows, preferred_element_type=jnp.float32
    ) * head_dim ** (-0.5)
    weights = (
        jnp.where(allowed[None], jax.nn.silu(scores), 0.0)
        / spread.astype(jnp.float32)[None, :, None]
    )
    weights = weights.astype(jnp.bfloat16)
    attended = jnp.einsum(
        "hqk,khd->qhd", weights, values, preferred_element_type=jnp.float32
    ).reshape(row_count, model_width)
    average = jnp.mean(attended, axis=1, keepdims=True)
    centered = attended - average
    variance = jnp.mean(centered * centered, axis=1, keepdims=True)
    gating = balanced[:, 3 * model_width : 4 * model_width].astype(jnp.float32)
    return (centered * lax.rsqrt(variance + 1e-05) * gating).astype(jnp.bfloat16)


def gate_share(normed, router, routes):
    logits = jnp.dot(normed, router, preferred_element_type=jnp.float32)
    scores = jax.nn.sigmoid(logits)
    picked = routes[:, :, None] == jnp.arange(router.shape[1], dtype=jnp.int32)[None, None, :]
    chosen = jnp.sum(jnp.where(picked, scores[:, None, :], 0.0), axis=2)
    return chosen / jnp.sum(chosen, axis=1, keepdims=True)


def pair_slots(routes, capacity):
    chosen = routes.reshape(-1)
    order = jnp.arange(chosen.shape[0], dtype=jnp.int32)
    same = (chosen[:, None] == chosen[None, :]) & (order[None, :] < order[:, None])
    ranking = jnp.sum(same.astype(jnp.int32), axis=1)
    return (chosen * capacity + ranking).reshape(routes.shape)


def per_row(pages, page_rows):
    return jnp.broadcast_to(pages[:, None], (pages.shape[0], page_rows)).reshape(-1)


def half_expert(rows, gate_cols, up_cols, down_rows):
    gate_act = jnp.dot(rows, gate_cols, preferred_element_type=jnp.float32)
    up_act = jnp.dot(rows, up_cols, preferred_element_type=jnp.float32)
    hidden = (jax.nn.silu(gate_act) * up_act).astype(jnp.bfloat16)
    return jnp.dot(hidden, down_rows, preferred_element_type=jnp.float32).astype(jnp.bfloat16)


def gathered_projection(block):
    devices = lax.axis_size("expert")
    groups = [list(range(first, devices, 2)) for first in range(2)]
    own = lax.all_gather(block, "expert", axis_index_groups=groups)
    return own, swapped(own, "expert", 0)


def shards(histories, page_map, user_pages, tails, routes, out_proj, router, w_gate, w_up, w_down):
    devices = lax.axis_size("expert")
    parity = lax.axis_index("expert") % 2
    own_proj, other_proj = gathered_projection(out_proj[0])
    other_gate = swapped(w_gate[0], "expert", 0)
    other_up = swapped(w_up[0], "expert", 0)
    other_down = swapped(w_down[0], "expert", 0)
    row_count = histories.shape[1]
    stacked_width = histories.shape[2]
    model_width = stacked_width // 5
    pages_dev = page_map.shape[2]
    page_rows = row_count // pages_dev
    page_slots = (pages_dev + devices - 1) // devices
    target = page_map[0, 0]
    target_dev = target // pages_dev
    earlier = (target_dev[None, :] == target_dev[:, None]) & (target[None, :] < target[:, None])
    position = target_dev * page_slots + jnp.sum(earlier.astype(jnp.int32), axis=1)
    sent_count = devices * page_slots * page_rows
    source_row = jnp.arange(row_count, dtype=jnp.int32)
    wire_row = jnp.arange(sent_count, dtype=jnp.int32)
    goes_to = per_row(position, page_rows) * page_rows + source_row % page_rows
    placing = (wire_row[:, None] == goes_to[None, :]).astype(jnp.bfloat16)
    outgoing = jnp.dot(placing, histories[0])
    arrived = lax.all_to_all(outgoing, "expert", split_axis=0, concat_axis=0, tiled=True)
    anchor = page_map[0, 1]
    anchor_dev = anchor // pages_dev
    ordering = jnp.arange(pages_dev, dtype=jnp.int32)
    sooner = (anchor_dev[None, :] == anchor_dev[:, None]) & (ordering[None, :] < ordering[:, None])
    where_from = anchor_dev * page_slots + jnp.sum(sooner.astype(jnp.int32), axis=1)
    comes_from = per_row(where_from, page_rows) * page_rows + source_row % page_rows
    taking = (comes_from[:, None] == wire_row[None, :]).astype(jnp.bfloat16)
    balanced = jnp.dot(taking, arrived)
    mixed_in = attend(balanced, user_pages[0, 0], tails[0, 0], page_rows)
    is_odd = parity == 1
    even_odd = mixed_in.reshape(row_count, devices // 2, 2, out_proj.shape[1])
    even = even_odd[:, :, 0].reshape(row_count, -1)
    odd = even_odd[:, :, 1].reshape(row_count, -1)
    own_mixed = jnp.where(is_odd, odd, even)
    other_mixed = jnp.where(is_odd, even, odd)
    projected = jnp.dot(
        own_mixed, own_proj.reshape(-1, model_width), preferred_element_type=jnp.float32
    ) + jnp.dot(
        other_mixed, other_proj.reshape(-1, model_width), preferred_element_type=jnp.float32
    )
    resid = (balanced[:, 4 * model_width :].astype(jnp.float32) + projected).astype(jnp.bfloat16)
    resid_wide = resid.astype(jnp.float32)
    normed = (
        resid_wide * lax.rsqrt(jnp.mean(resid_wide * resid_wide, axis=1, keepdims=True) + 1e-06)
    ).astype(jnp.bfloat16)
    experts = router.shape[2]
    capacity = 4 * row_count // experts
    share = gate_share(normed, router[0], routes[0])
    slots = pair_slots(routes[0], capacity)
    slot_index = jnp.arange(experts * capacity, dtype=jnp.int32)
    packing = (
        (slots[None, :, 0] == slot_index[:, None]) | (slots[None, :, 1] == slot_index[:, None])
    ).astype(jnp.bfloat16)
    packed = jnp.dot(packing, normed)
    own_rows = lax.all_to_all(packed, "expert", split_axis=0, concat_axis=0, tiled=True)
    own_part = half_expert(own_rows, w_gate[0], w_up[0], w_down[0])
    other_part = half_expert(own_rows, other_gate, other_up, other_down)
    served = (own_part.astype(jnp.float32) + other_part.astype(jnp.float32)).astype(jnp.bfloat16)
    came_back = lax.all_to_all(served, "expert", split_axis=0, concat_axis=0, tiled=True)
    mixture = jnp.zeros_like(resid_wide)
    for k in range(slots.shape[1]):
        picking = (slots[:, k : k + 1] == slot_index[None, :]).astype(jnp.bfloat16)
        picked = jnp.dot(picking, came_back, preferred_element_type=jnp.float32)
        mixture = mixture + picked * share[:, k : k + 1]
    output_rows = (resid_wide + mixture).astype(jnp.bfloat16)
    return from_behind(output_rows[None], "section", 1)


def solution(mesh):
    in_specs = (
        P("section", "expert", None),
        P("section", None, "expert"),
        P("section", "expert", None),
        P("section", "expert", None),
        P("section", "expert", None),
        P("section", "expert", None),
        P("section", None, None),
        P("section", None, "expert"),
        P("section", None, "expert"),
        P("section", "expert", None),
    )
    out_specs = P("section", "expert", None)
    return jax.shard_map(shards, mesh=mesh, in_specs=in_specs, out_specs=out_specs, check_vma=False)
```

```python
import jax
import jax.numpy as jnp
from jax import lax
from jax.experimental import pallas as pl
from jax.experimental.pallas import tpu as pltpu
from jax.sharding import PartitionSpec as P

HEADS = 8


def swapped(shard, axis, apart):
    return lax.ppermute(shard, axis, [(i, i ^ 1 << apart) for i in range(lax.axis_size(axis))])


def from_behind(block, axis, distance):
    devices = range(lax.axis_size(axis))
    route = [((i - distance) % len(devices), i) for i in devices]
    return lax.ppermute(block, axis, route)


def layout_rows(counts, tail_rows, page_rows, row_count):
    member_index = jnp.arange(counts.shape[0], dtype=jnp.int32)
    ahead = member_index[None, :] < member_index[:, None]
    starting = jnp.sum(jnp.where(ahead, counts[None, :], 0), axis=1)
    length = (counts - 1) * page_rows + tail_rows
    row_index = jnp.arange(row_count, dtype=jnp.int32)
    page_of = row_index // page_rows
    owner_of = jnp.sum((starting[None, :] <= page_of[:, None]).astype(jnp.int32), axis=1) - 1
    member = owner_of[:, None] == jnp.arange(counts.shape[0], dtype=jnp.int32)[None, :]
    offset = jnp.sum(jnp.where(member, starting[None, :] * page_rows, 0), axis=1)
    spread = jnp.sum(jnp.where(member, length[None, :], 0), axis=1)
    return (owner_of, row_index - offset, spread)


def attend(balanced, counts, tail_rows, page_rows):
    row_count = balanced.shape[0]
    model_width = balanced.shape[1] // 5
    head_dim = model_width // HEADS
    owner_of, position, spread = layout_rows(counts, tail_rows, page_rows, row_count)
    allowed = (
        (owner_of[:, None] == owner_of[None, :])
        & (position[None, :] <= position[:, None])
        & (position[None, :] < spread[None, :])
    )
    queries = balanced[:, :model_width].reshape(row_count, HEADS, head_dim)
    key_rows = balanced[:, model_width : 2 * model_width].reshape(row_count, HEADS, head_dim)
    values = balanced[:, 2 * model_width : 3 * model_width].reshape(row_count, HEADS, head_dim)
    scores = jnp.einsum(
        "qhd,khd->hqk", queries, key_rows, preferred_element_type=jnp.float32
    ) * head_dim ** (-0.5)
    weights = (
        jnp.where(allowed[None], jax.nn.silu(scores), 0.0)
        / spread.astype(jnp.float32)[None, :, None]
    )
    weights = weights.astype(jnp.bfloat16)
    attended = jnp.einsum(
        "hqk,khd->qhd", weights, values, preferred_element_type=jnp.float32
    ).reshape(row_count, model_width)
    average = jnp.mean(attended, axis=1, keepdims=True)
    centered = attended - average
    variance = jnp.mean(centered * centered, axis=1, keepdims=True)
    gating = balanced[:, 3 * model_width : 4 * model_width].astype(jnp.float32)
    return (centered * lax.rsqrt(variance + 1e-05) * gating).astype(jnp.bfloat16)


def gate_share(normed, router, routes):
    logits = jnp.dot(normed, router, preferred_element_type=jnp.float32)
    scores = jax.nn.sigmoid(logits)
    picked = routes[:, :, None] == jnp.arange(router.shape[1], dtype=jnp.int32)[None, None, :]
    chosen = jnp.sum(jnp.where(picked, scores[:, None, :], 0.0), axis=2)
    return chosen / jnp.sum(chosen, axis=1, keepdims=True)


def pair_slots(routes, capacity):
    chosen = routes.reshape(-1)
    order = jnp.arange(chosen.shape[0], dtype=jnp.int32)
    same = (chosen[:, None] == chosen[None, :]) & (order[None, :] < order[:, None])
    ranking = jnp.sum(same.astype(jnp.int32), axis=1)
    return (chosen * capacity + ranking).reshape(routes.shape)


def per_row(pages, page_rows):
    return jnp.broadcast_to(pages[:, None], (pages.shape[0], page_rows)).reshape(-1)


def expert_kernel(rows_ref, gate0, up0, down0, gate1, up1, down1, out_ref, hidden_ref):
    units = gate0.shape[1]
    tile = 256 if units % 256 == 0 else units
    for half, (gate_ref, up_ref, down_ref) in enumerate(((gate0, up0, down0), (gate1, up1, down1))):
        for first in range(0, units, tile):
            span = slice(first, first + tile)
            gate_act = jnp.dot(
                rows_ref[...], gate_ref[:, span], preferred_element_type=jnp.float32
            )
            up_act = jnp.dot(rows_ref[...], up_ref[:, span], preferred_element_type=jnp.float32)
            hidden_ref[:, span] = (jax.nn.silu(gate_act) * up_act).astype(jnp.bfloat16)
        for first in range(0, out_ref.shape[1], tile):
            span = slice(first, first + tile)
            part = jnp.dot(
                hidden_ref[...], down_ref[:, span], preferred_element_type=jnp.float32
            ).astype(jnp.bfloat16)
            if half == 0:
                out_ref[:, span] = part
            else:
                earlier = out_ref[:, span].astype(jnp.float32)
                out_ref[:, span] = (earlier + part.astype(jnp.float32)).astype(jnp.bfloat16)


def whole_expert(rows, *weights):
    count, width = rows.shape
    units = weights[0].shape[1]
    return pl.pallas_call(
        expert_kernel,
        out_shape=jax.ShapeDtypeStruct((count, width), jnp.bfloat16),
        in_specs=[pl.BlockSpec(memory_space=pltpu.VMEM)] * 7,
        out_specs=pl.BlockSpec(memory_space=pltpu.VMEM),
        scratch_shapes=[pltpu.VMEM((count, units), jnp.bfloat16)],
        compiler_params=pltpu.CompilerParams(vmem_limit_bytes=32 * 1024 * 1024),
        cost_estimate=pl.CostEstimate(
            flops=12 * count * width * units,
            bytes_accessed=12 * width * units + 4 * count * width,
            transcendentals=2 * count * units,
        ),
        name="expert_pair",
    )(rows, *weights)


def gathered_projection(block):
    devices = lax.axis_size("expert")
    me = lax.axis_index("expert")
    rows = block.shape[0]
    line = [block] + [from_behind(block, "expert", 4 * k) for k in range(1, devices // 4)]
    line = jnp.concatenate(line, axis=0)
    plane = jnp.concatenate([line, swapped(line, "expert", 1)], axis=0)
    other = swapped(plane, "expert", 0)
    slot = jnp.arange(devices * rows, dtype=jnp.int32)
    turn, inner = slot // rows, slot % rows
    steps = turn % (devices // 4)
    side = (turn // (devices // 4)) % 2
    core = turn // (devices // 2)
    line_at = (me // 4 - steps + devices // 4) % (devices // 4)
    side_at = (me // 2 + side) % 2
    core_at = (me + core) % 2
    return plane, other, (line_at * 4 + side_at * 2 + core_at) * rows + inner


def shards(histories, page_map, user_pages, tails, routes, out_proj, router, w_gate, w_up, w_down):
    devices = lax.axis_size("expert")
    own_proj, other_proj, proj_row = gathered_projection(out_proj[0])
    other_gate = swapped(w_gate[0], "expert", 0)
    other_up = swapped(w_up[0], "expert", 0)
    other_down = swapped(w_down[0], "expert", 0)
    row_count = histories.shape[1]
    stacked_width = histories.shape[2]
    model_width = stacked_width // 5
    pages_dev = page_map.shape[2]
    page_rows = row_count // pages_dev
    page_slots = (pages_dev + devices - 1) // devices
    target = page_map[0, 0]
    target_dev = target // pages_dev
    earlier = (target_dev[None, :] == target_dev[:, None]) & (target[None, :] < target[:, None])
    position = target_dev * page_slots + jnp.sum(earlier.astype(jnp.int32), axis=1)
    sent_count = devices * page_slots * page_rows
    source_row = jnp.arange(row_count, dtype=jnp.int32)
    wire_row = jnp.arange(sent_count, dtype=jnp.int32)
    goes_to = per_row(position, page_rows) * page_rows + source_row % page_rows
    placing = (wire_row[:, None] == goes_to[None, :]).astype(jnp.bfloat16)
    outgoing = jnp.dot(placing, histories[0])
    arrived = lax.all_to_all(outgoing, "expert", split_axis=0, concat_axis=0, tiled=True)
    anchor = page_map[0, 1]
    anchor_dev = anchor // pages_dev
    ordering = jnp.arange(pages_dev, dtype=jnp.int32)
    sooner = (anchor_dev[None, :] == anchor_dev[:, None]) & (ordering[None, :] < ordering[:, None])
    where_from = anchor_dev * page_slots + jnp.sum(sooner.astype(jnp.int32), axis=1)
    comes_from = per_row(where_from, page_rows) * page_rows + source_row % page_rows
    taking = (comes_from[:, None] == wire_row[None, :]).astype(jnp.bfloat16)
    balanced = jnp.dot(taking, arrived)
    mixed_in = attend(balanced, user_pages[0, 0], tails[0, 0], page_rows)
    columns = jnp.arange(model_width, dtype=jnp.int32)
    ordering_of = (columns[:, None] == proj_row[None, :]).astype(jnp.bfloat16)
    ordered = jnp.dot(mixed_in, ordering_of)
    own_mixed, other_mixed = ordered[:, : model_width // 2], ordered[:, model_width // 2 :]
    projected = jnp.dot(
        own_mixed, own_proj, preferred_element_type=jnp.float32
    ) + jnp.dot(
        other_mixed, other_proj, preferred_element_type=jnp.float32
    )
    resid = (balanced[:, 4 * model_width :].astype(jnp.float32) + projected).astype(jnp.bfloat16)
    resid_wide = resid.astype(jnp.float32)
    normed = (
        resid_wide * lax.rsqrt(jnp.mean(resid_wide * resid_wide, axis=1, keepdims=True) + 1e-06)
    ).astype(jnp.bfloat16)
    experts = router.shape[2]
    capacity = 4 * row_count // experts
    share = gate_share(normed, router[0], routes[0])
    slots = pair_slots(routes[0], capacity)
    slot_index = jnp.arange(experts * capacity, dtype=jnp.int32)
    packing = (
        (slots[None, :, 0] == slot_index[:, None]) | (slots[None, :, 1] == slot_index[:, None])
    ).astype(jnp.bfloat16)
    packed = jnp.dot(packing, normed)
    own_rows = lax.all_to_all(packed, "expert", split_axis=0, concat_axis=0, tiled=True)
    served = whole_expert(
        own_rows, w_gate[0], w_up[0], w_down[0], other_gate, other_up, other_down
    )
    came_back = lax.all_to_all(served, "expert", split_axis=0, concat_axis=0, tiled=True)
    mixture = jnp.zeros_like(resid_wide)
    for k in range(slots.shape[1]):
        picking = (slots[:, k : k + 1] == slot_index[None, :]).astype(jnp.bfloat16)
        picked = jnp.dot(picking, came_back, preferred_element_type=jnp.float32)
        mixture = mixture + picked * share[:, k : k + 1]
    output_rows = (resid_wide + mixture).astype(jnp.bfloat16)
    return from_behind(output_rows[None], "section", 1)


def solution(mesh):
    in_specs = (
        P("section", "expert", None),
        P("section", None, "expert"),
        P("section", "expert", None),
        P("section", "expert", None),
        P("section", "expert", None),
        P("section", "expert", None),
        P("section", None, None),
        P("section", None, "expert"),
        P("section", None, "expert"),
        P("section", "expert", None),
    )
    out_specs = P("section", "expert", None)
    return jax.shard_map(shards, mesh=mesh, in_specs=in_specs, out_specs=out_specs, check_vma=False)
```

```python
import jax
import jax.numpy as jnp
from jax import lax
from jax.experimental import pallas as pl
from jax.experimental.pallas import tpu as pltpu
from jax.sharding import PartitionSpec as P

HEADS = 8


def swapped(shard, axis, apart):
    return lax.ppermute(shard, axis, [(i, i ^ 1 << apart) for i in range(lax.axis_size(axis))])


def from_behind(block, axis, distance):
    devices = range(lax.axis_size(axis))
    route = [((i - distance) % len(devices), i) for i in devices]
    return lax.ppermute(block, axis, route)


def layout_rows(counts, tail_rows, page_rows, row_count):
    member_index = jnp.arange(counts.shape[0], dtype=jnp.int32)
    ahead = member_index[None, :] < member_index[:, None]
    starting = jnp.sum(jnp.where(ahead, counts[None, :], 0), axis=1)
    length = (counts - 1) * page_rows + tail_rows
    row_index = jnp.arange(row_count, dtype=jnp.int32)
    page_of = row_index // page_rows
    owner_of = jnp.sum((starting[None, :] <= page_of[:, None]).astype(jnp.int32), axis=1) - 1
    member = owner_of[:, None] == jnp.arange(counts.shape[0], dtype=jnp.int32)[None, :]
    offset = jnp.sum(jnp.where(member, starting[None, :] * page_rows, 0), axis=1)
    spread = jnp.sum(jnp.where(member, length[None, :], 0), axis=1)
    return (owner_of, row_index - offset, spread)


def attend(balanced, counts, tail_rows, page_rows):
    row_count = balanced.shape[0]
    model_width = balanced.shape[1] // 5
    head_dim = model_width // HEADS
    owner_of, position, spread = layout_rows(counts, tail_rows, page_rows, row_count)
    allowed = (
        (owner_of[:, None] == owner_of[None, :])
        & (position[None, :] <= position[:, None])
        & (position[None, :] < spread[None, :])
    )
    queries = balanced[:, :model_width].reshape(row_count, HEADS, head_dim)
    key_rows = balanced[:, model_width : 2 * model_width].reshape(row_count, HEADS, head_dim)
    values = balanced[:, 2 * model_width : 3 * model_width].reshape(row_count, HEADS, head_dim)
    scores = jnp.einsum(
        "qhd,khd->hqk", queries, key_rows, preferred_element_type=jnp.float32
    ) * head_dim ** (-0.5)
    weights = (
        jnp.where(allowed[None], jax.nn.silu(scores), 0.0)
        / spread.astype(jnp.float32)[None, :, None]
    )
    weights = weights.astype(jnp.bfloat16)
    attended = jnp.einsum(
        "hqk,khd->qhd", weights, values, preferred_element_type=jnp.float32
    ).reshape(row_count, model_width)
    average = jnp.mean(attended, axis=1, keepdims=True)
    centered = attended - average
    variance = jnp.mean(centered * centered, axis=1, keepdims=True)
    gating = balanced[:, 3 * model_width : 4 * model_width].astype(jnp.float32)
    return (centered * lax.rsqrt(variance + 1e-05) * gating).astype(jnp.bfloat16)


def gate_share(normed, router, routes):
    logits = jnp.dot(normed, router, preferred_element_type=jnp.float32)
    scores = jax.nn.sigmoid(logits)
    picked = routes[:, :, None] == jnp.arange(router.shape[1], dtype=jnp.int32)[None, None, :]
    chosen = jnp.sum(jnp.where(picked, scores[:, None, :], 0.0), axis=2)
    return chosen / jnp.sum(chosen, axis=1, keepdims=True)


def pair_slots(routes, capacity):
    chosen = routes.reshape(-1)
    order = jnp.arange(chosen.shape[0], dtype=jnp.int32)
    same = (chosen[:, None] == chosen[None, :]) & (order[None, :] < order[:, None])
    ranking = jnp.sum(same.astype(jnp.int32), axis=1)
    return (chosen * capacity + ranking).reshape(routes.shape)


def per_row(pages, page_rows):
    return jnp.broadcast_to(pages[:, None], (pages.shape[0], page_rows)).reshape(-1)


def expert_kernel(rows_ref, *refs):
    stored, (out_ref, hidden_ref), held, arrival = refs[:6], refs[6:8], refs[8:14], refs[14]
    loads = [
        pltpu.make_async_copy(there, here, arrival.at[i])
        for i, (there, here) in enumerate(zip(stored, held))
    ]
    for load in loads:
        load.start()
    units = stored[0].shape[1]
    tile = 256 if units % 256 == 0 else units
    for half in range(2):
        gate_ref, up_ref, down_ref = held[3 * half : 3 * half + 3]
        loads[3 * half].wait()
        loads[3 * half + 1].wait()
        for first in range(0, units, tile):
            span = slice(first, first + tile)
            gate_act = jnp.dot(
                rows_ref[...], gate_ref[:, span], preferred_element_type=jnp.float32
            )
            up_act = jnp.dot(rows_ref[...], up_ref[:, span], preferred_element_type=jnp.float32)
            hidden_ref[:, span] = (jax.nn.silu(gate_act) * up_act).astype(jnp.bfloat16)
        loads[3 * half + 2].wait()
        for first in range(0, out_ref.shape[1], tile):
            span = slice(first, first + tile)
            part = jnp.dot(
                hidden_ref[...], down_ref[:, span], preferred_element_type=jnp.float32
            ).astype(jnp.bfloat16)
            if half == 0:
                out_ref[:, span] = part
            else:
                earlier = out_ref[:, span].astype(jnp.float32)
                out_ref[:, span] = (earlier + part.astype(jnp.float32)).astype(jnp.bfloat16)


def whole_expert(rows, *weights):
    count, width = rows.shape
    units = weights[0].shape[1]
    return pl.pallas_call(
        expert_kernel,
        out_shape=jax.ShapeDtypeStruct((count, width), jnp.bfloat16),
        in_specs=[pl.BlockSpec(memory_space=pltpu.VMEM)]
        + [pl.BlockSpec(memory_space=pl.ANY)] * 6,
        out_specs=pl.BlockSpec(memory_space=pltpu.VMEM),
        scratch_shapes=[pltpu.VMEM((count, units), jnp.bfloat16)]
        + [pltpu.VMEM(weight.shape, weight.dtype) for weight in weights]
        + [pltpu.SemaphoreType.DMA((len(weights),))],
        compiler_params=pltpu.CompilerParams(vmem_limit_bytes=54 * 1024 * 1024),
        cost_estimate=pl.CostEstimate(
            flops=12 * count * width * units,
            bytes_accessed=12 * width * units + 4 * count * width,
            transcendentals=2 * count * units,
        ),
        name="expert_pair",
    )(rows, *weights)


def gathered_projection(block):
    devices = lax.axis_size("expert")
    me = lax.axis_index("expert")
    rows = block.shape[0]
    line = [block] + [from_behind(block, "expert", 4 * k) for k in range(1, devices // 4)]
    line = jnp.concatenate(line, axis=0)
    plane = jnp.concatenate([line, swapped(line, "expert", 1)], axis=0)
    other = swapped(plane, "expert", 0)
    slot = jnp.arange(devices * rows, dtype=jnp.int32)
    turn, inner = slot // rows, slot % rows
    steps = turn % (devices // 4)
    side = (turn // (devices // 4)) % 2
    core = turn // (devices // 2)
    line_at = (me // 4 - steps + devices // 4) % (devices // 4)
    side_at = (me // 2 + side) % 2
    core_at = (me + core) % 2
    return plane, other, (line_at * 4 + side_at * 2 + core_at) * rows + inner


def shards(histories, page_map, user_pages, tails, routes, out_proj, router, w_gate, w_up, w_down):
    devices = lax.axis_size("expert")
    own_proj, other_proj, proj_row = gathered_projection(out_proj[0])
    other_gate = swapped(w_gate[0], "expert", 0)
    other_up = swapped(w_up[0], "expert", 0)
    other_down = swapped(w_down[0], "expert", 0)
    row_count = histories.shape[1]
    stacked_width = histories.shape[2]
    model_width = stacked_width // 5
    pages_dev = page_map.shape[2]
    page_rows = row_count // pages_dev
    page_slots = (pages_dev + devices - 1) // devices
    target = page_map[0, 0]
    target_dev = target // pages_dev
    earlier = (target_dev[None, :] == target_dev[:, None]) & (target[None, :] < target[:, None])
    position = target_dev * page_slots + jnp.sum(earlier.astype(jnp.int32), axis=1)
    sent_count = devices * page_slots * page_rows
    source_row = jnp.arange(row_count, dtype=jnp.int32)
    wire_row = jnp.arange(sent_count, dtype=jnp.int32)
    goes_to = per_row(position, page_rows) * page_rows + source_row % page_rows
    placing = (wire_row[:, None] == goes_to[None, :]).astype(jnp.bfloat16)
    outgoing = jnp.dot(placing, histories[0])
    arrived = lax.all_to_all(outgoing, "expert", split_axis=0, concat_axis=0, tiled=True)
    anchor = page_map[0, 1]
    anchor_dev = anchor // pages_dev
    ordering = jnp.arange(pages_dev, dtype=jnp.int32)
    sooner = (anchor_dev[None, :] == anchor_dev[:, None]) & (ordering[None, :] < ordering[:, None])
    where_from = anchor_dev * page_slots + jnp.sum(sooner.astype(jnp.int32), axis=1)
    comes_from = per_row(where_from, page_rows) * page_rows + source_row % page_rows
    taking = (comes_from[:, None] == wire_row[None, :]).astype(jnp.bfloat16)
    balanced = jnp.dot(taking, arrived)
    mixed_in = attend(balanced, user_pages[0, 0], tails[0, 0], page_rows)
    columns = jnp.arange(model_width, dtype=jnp.int32)
    ordering_of = (columns[:, None] == proj_row[None, :]).astype(jnp.bfloat16)
    ordered = jnp.dot(mixed_in, ordering_of)
    own_mixed, other_mixed = ordered[:, : model_width // 2], ordered[:, model_width // 2 :]
    projected = jnp.dot(
        own_mixed, own_proj, preferred_element_type=jnp.float32
    ) + jnp.dot(
        other_mixed, other_proj, preferred_element_type=jnp.float32
    )
    resid = (balanced[:, 4 * model_width :].astype(jnp.float32) + projected).astype(jnp.bfloat16)
    resid_wide = resid.astype(jnp.float32)
    normed = (
        resid_wide * lax.rsqrt(jnp.mean(resid_wide * resid_wide, axis=1, keepdims=True) + 1e-06)
    ).astype(jnp.bfloat16)
    experts = router.shape[2]
    capacity = 4 * row_count // experts
    share = gate_share(normed, router[0], routes[0])
    slots = pair_slots(routes[0], capacity)
    slot_index = jnp.arange(experts * capacity, dtype=jnp.int32)
    packing = (
        (slots[None, :, 0] == slot_index[:, None]) | (slots[None, :, 1] == slot_index[:, None])
    ).astype(jnp.bfloat16)
    packed = jnp.dot(packing, normed)
    own_rows = lax.all_to_all(packed, "expert", split_axis=0, concat_axis=0, tiled=True)
    served = whole_expert(
        own_rows, w_gate[0], w_up[0], w_down[0], other_gate, other_up, other_down
    )
    came_back = lax.all_to_all(served, "expert", split_axis=0, concat_axis=0, tiled=True)
    mixture = jnp.zeros_like(resid_wide)
    for k in range(slots.shape[1]):
        picking = (slots[:, k : k + 1] == slot_index[None, :]).astype(jnp.bfloat16)
        picked = jnp.dot(picking, came_back, preferred_element_type=jnp.float32)
        mixture = mixture + picked * share[:, k : k + 1]
    output_rows = (resid_wide + mixture).astype(jnp.bfloat16)
    return from_behind(output_rows[None], "section", 1)


def solution(mesh):
    in_specs = (
        P("section", "expert", None),
        P("section", None, "expert"),
        P("section", "expert", None),
        P("section", "expert", None),
        P("section", "expert", None),
        P("section", "expert", None),
        P("section", None, None),
        P("section", None, "expert"),
        P("section", None, "expert"),
        P("section", "expert", None),
    )
    out_specs = P("section", "expert", None)
    return jax.shard_map(shards, mesh=mesh, in_specs=in_specs, out_specs=out_specs, check_vma=False)
```

```python
import functools

import jax
import jax.numpy as jnp
from jax import lax
from jax.experimental import pallas as pl
from jax.experimental.pallas import tpu as pltpu
from jax.sharding import PartitionSpec as P

HEADS = 8


def swapped(shard, axis, apart):
    return lax.ppermute(shard, axis, [(i, i ^ 1 << apart) for i in range(lax.axis_size(axis))])


def from_behind(block, axis, distance):
    devices = range(lax.axis_size(axis))
    route = [((i - distance) % len(devices), i) for i in devices]
    return lax.ppermute(block, axis, route)


def layout_rows(counts, tail_rows, page_rows, row_count):
    member_index = jnp.arange(counts.shape[0], dtype=jnp.int32)
    ahead = member_index[None, :] < member_index[:, None]
    starting = jnp.sum(jnp.where(ahead, counts[None, :], 0), axis=1)
    length = (counts - 1) * page_rows + tail_rows
    row_index = jnp.arange(row_count, dtype=jnp.int32)
    page_of = row_index // page_rows
    owner_of = jnp.sum((starting[None, :] <= page_of[:, None]).astype(jnp.int32), axis=1) - 1
    member = owner_of[:, None] == jnp.arange(counts.shape[0], dtype=jnp.int32)[None, :]
    offset = jnp.sum(jnp.where(member, starting[None, :] * page_rows, 0), axis=1)
    spread = jnp.sum(jnp.where(member, length[None, :], 0), axis=1)
    return (owner_of, row_index - offset, spread)


def attend(balanced, counts, tail_rows, page_rows):
    row_count = balanced.shape[0]
    model_width = balanced.shape[1] // 5
    head_dim = model_width // HEADS
    owner_of, position, spread = layout_rows(counts, tail_rows, page_rows, row_count)
    allowed = (
        (owner_of[:, None] == owner_of[None, :])
        & (position[None, :] <= position[:, None])
        & (position[None, :] < spread[None, :])
    )
    queries = balanced[:, :model_width].reshape(row_count, HEADS, head_dim)
    key_rows = balanced[:, model_width : 2 * model_width].reshape(row_count, HEADS, head_dim)
    values = balanced[:, 2 * model_width : 3 * model_width].reshape(row_count, HEADS, head_dim)
    scores = jnp.einsum(
        "qhd,khd->hqk", queries, key_rows, preferred_element_type=jnp.float32
    ) * head_dim ** (-0.5)
    weights = (
        jnp.where(allowed[None], jax.nn.silu(scores), 0.0)
        / spread.astype(jnp.float32)[None, :, None]
    )
    weights = weights.astype(jnp.bfloat16)
    attended = jnp.einsum(
        "hqk,khd->qhd", weights, values, preferred_element_type=jnp.float32
    ).reshape(row_count, model_width)
    average = jnp.mean(attended, axis=1, keepdims=True)
    centered = attended - average
    variance = jnp.mean(centered * centered, axis=1, keepdims=True)
    gating = balanced[:, 3 * model_width : 4 * model_width].astype(jnp.float32)
    return (centered * lax.rsqrt(variance + 1e-05) * gating).astype(jnp.bfloat16)


def gate_share(normed, router, routes):
    logits = jnp.dot(normed, router, preferred_element_type=jnp.float32)
    scores = jax.nn.sigmoid(logits)
    picked = routes[:, :, None] == jnp.arange(router.shape[1], dtype=jnp.int32)[None, None, :]
    chosen = jnp.sum(jnp.where(picked, scores[:, None, :], 0.0), axis=2)
    return chosen / jnp.sum(chosen, axis=1, keepdims=True)


def pair_slots(routes, capacity):
    chosen = routes.reshape(-1)
    order = jnp.arange(chosen.shape[0], dtype=jnp.int32)
    same = (chosen[:, None] == chosen[None, :]) & (order[None, :] < order[:, None])
    ranking = jnp.sum(same.astype(jnp.int32), axis=1)
    return (chosen * capacity + ranking).reshape(routes.shape)


def per_row(pages, page_rows):
    return jnp.broadcast_to(pages[:, None], (pages.shape[0], page_rows)).reshape(-1)


def expert_kernel(devices, packed_ref, *refs):
    stored, (back_ref, rows_ref, served_ref, hidden_ref), held = refs[:6], refs[6:10], refs[10:16]
    arrival, own_sem, send_sem, recv_sem = refs[16:]
    me = lax.axis_index("expert")
    loads = [
        pltpu.make_async_copy(there, here, arrival.at[i])
        for i, (there, here) in enumerate(zip(stored, held))
    ]
    for load in loads:
        load.start()

    def each_peer(first, last, action):
        def step(peer, carry):
            @pl.when(peer != me)
            def _():
                action(peer)

            return carry

        lax.fori_loop(first, last, step, 0)

    def transfer(source, target, hop, peer, sender):
        return pltpu.make_async_remote_copy(
            src_ref=source,
            dst_ref=target,
            send_sem=send_sem.at[hop, peer],
            recv_sem=recv_sem.at[hop, sender],
            device_id={"expert": peer},
            device_id_type=pl.DeviceIdType.MESH,
        )

    def out_to(peer):
        return transfer(packed_ref.at[peer], rows_ref.at[me], 0, peer, me)

    def back_to(peer):
        return transfer(served_ref.at[peer], back_ref.at[me], 1, peer, me)

    barrier = pltpu.get_barrier_semaphore()
    each_peer(
        0,
        devices,
        lambda peer: pl.semaphore_signal(
            barrier, inc=1, device_id={"expert": peer}, device_id_type=pl.DeviceIdType.MESH
        ),
    )
    pl.semaphore_wait(barrier, devices - 1)
    each_peer(0, devices, lambda peer: out_to(peer).start())
    kept = pltpu.make_async_copy(packed_ref.at[me], rows_ref.at[me], own_sem.at[0])
    kept.start()
    kept.wait()
    units = stored[0].shape[1]
    width = packed_ref.shape[2]
    tile = 256 if units % 256 == 0 else units
    group = devices // 2
    for turn in range(2):
        begin = turn * group
        each_peer(
            begin,
            begin + group,
            lambda peer: transfer(packed_ref.at[peer], rows_ref.at[peer], 0, peer, peer).wait_recv(),
        )
        rows = rows_ref[begin : begin + group].reshape(-1, width)
        for half in range(2):
            gate_ref, up_ref, down_ref = held[3 * half : 3 * half + 3]
            if turn == 0:
                loads[3 * half].wait()
                loads[3 * half + 1].wait()
            for first in range(0, units, tile):
                span = slice(first, first + tile)
                gate_act = jnp.dot(rows, gate_ref[:, span], preferred_element_type=jnp.float32)
                up_act = jnp.dot(rows, up_ref[:, span], preferred_element_type=jnp.float32)
                hidden_ref[:, span] = (jax.nn.silu(gate_act) * up_act).astype(jnp.bfloat16)
            if turn == 0:
                loads[3 * half + 2].wait()
            for first in range(0, width, tile):
                span = slice(first, first + tile)
                part = jnp.dot(
                    hidden_ref[...], down_ref[:, span], preferred_element_type=jnp.float32
                ).astype(jnp.bfloat16)
                part = part.reshape(group, -1, tile)
                if half == 0:
                    served_ref[begin : begin + group, :, span] = part
                else:
                    earlier = served_ref[begin : begin + group, :, span].astype(jnp.float32)
                    served_ref[begin : begin + group, :, span] = (
                        earlier + part.astype(jnp.float32)
                    ).astype(jnp.bfloat16)
        each_peer(begin, begin + group, lambda peer: back_to(peer).start())
    kept = pltpu.make_async_copy(served_ref.at[me], back_ref.at[me], own_sem.at[1])
    kept.start()
    kept.wait()
    each_peer(0, devices, lambda peer: out_to(peer).wait_send())
    each_peer(0, devices, lambda peer: back_to(peer).wait_send())
    each_peer(
        0,
        devices,
        lambda peer: transfer(served_ref.at[peer], back_ref.at[peer], 1, peer, peer).wait_recv(),
    )


def exchanged_experts(packed, *weights):
    devices = lax.axis_size("expert")
    width = packed.shape[1]
    blocks = packed.reshape(devices, -1, width)
    count = packed.shape[0]
    units = weights[0].shape[1]
    came_back = pl.pallas_call(
        functools.partial(expert_kernel, devices),
        out_shape=jax.ShapeDtypeStruct(blocks.shape, jnp.bfloat16),
        in_specs=[pl.BlockSpec(memory_space=pltpu.VMEM)]
        + [pl.BlockSpec(memory_space=pl.ANY)] * 6,
        out_specs=pl.BlockSpec(memory_space=pltpu.VMEM),
        scratch_shapes=[
            pltpu.VMEM(blocks.shape, jnp.bfloat16),
            pltpu.VMEM(blocks.shape, jnp.bfloat16),
            pltpu.VMEM((count // 2, units), jnp.bfloat16),
        ]
        + [pltpu.VMEM(weight.shape, weight.dtype) for weight in weights]
        + [
            pltpu.SemaphoreType.DMA((len(weights),)),
            pltpu.SemaphoreType.DMA((2,)),
            pltpu.SemaphoreType.DMA((2, devices)),
            pltpu.SemaphoreType.DMA((2, devices)),
        ],
        compiler_params=pltpu.CompilerParams(
            vmem_limit_bytes=54 * 1024 * 1024, collective_id=0, has_side_effects=True
        ),
        cost_estimate=pl.CostEstimate(
            flops=12 * count * width * units,
            bytes_accessed=12 * width * units + 4 * count * width,
            transcendentals=2 * count * units,
        ),
        name="expert_exchange",
    )(blocks, *weights)
    return came_back.reshape(count, width)


def gathered_projection(block):
    devices = lax.axis_size("expert")
    me = lax.axis_index("expert")
    rows = block.shape[0]
    line = [block] + [from_behind(block, "expert", 4 * k) for k in range(1, devices // 4)]
    line = jnp.concatenate(line, axis=0)
    plane = jnp.concatenate([line, swapped(line, "expert", 1)], axis=0)
    other = swapped(plane, "expert", 0)
    slot = jnp.arange(devices * rows, dtype=jnp.int32)
    turn, inner = slot // rows, slot % rows
    steps = turn % (devices // 4)
    side = (turn // (devices // 4)) % 2
    core = turn // (devices // 2)
    line_at = (me // 4 - steps + devices // 4) % (devices // 4)
    side_at = (me // 2 + side) % 2
    core_at = (me + core) % 2
    return plane, other, (line_at * 4 + side_at * 2 + core_at) * rows + inner


def shards(histories, page_map, user_pages, tails, routes, out_proj, router, w_gate, w_up, w_down):
    devices = lax.axis_size("expert")
    own_proj, other_proj, proj_row = gathered_projection(out_proj[0])
    other_gate = swapped(w_gate[0], "expert", 0)
    other_up = swapped(w_up[0], "expert", 0)
    other_down = swapped(w_down[0], "expert", 0)
    row_count = histories.shape[1]
    stacked_width = histories.shape[2]
    model_width = stacked_width // 5
    pages_dev = page_map.shape[2]
    page_rows = row_count // pages_dev
    page_slots = (pages_dev + devices - 1) // devices
    target = page_map[0, 0]
    target_dev = target // pages_dev
    earlier = (target_dev[None, :] == target_dev[:, None]) & (target[None, :] < target[:, None])
    position = target_dev * page_slots + jnp.sum(earlier.astype(jnp.int32), axis=1)
    sent_count = devices * page_slots * page_rows
    source_row = jnp.arange(row_count, dtype=jnp.int32)
    wire_row = jnp.arange(sent_count, dtype=jnp.int32)
    goes_to = per_row(position, page_rows) * page_rows + source_row % page_rows
    placing = (wire_row[:, None] == goes_to[None, :]).astype(jnp.bfloat16)
    outgoing = jnp.dot(placing, histories[0])
    arrived = lax.all_to_all(outgoing, "expert", split_axis=0, concat_axis=0, tiled=True)
    anchor = page_map[0, 1]
    anchor_dev = anchor // pages_dev
    ordering = jnp.arange(pages_dev, dtype=jnp.int32)
    sooner = (anchor_dev[None, :] == anchor_dev[:, None]) & (ordering[None, :] < ordering[:, None])
    where_from = anchor_dev * page_slots + jnp.sum(sooner.astype(jnp.int32), axis=1)
    comes_from = per_row(where_from, page_rows) * page_rows + source_row % page_rows
    taking = (comes_from[:, None] == wire_row[None, :]).astype(jnp.bfloat16)
    balanced = jnp.dot(taking, arrived)
    mixed_in = attend(balanced, user_pages[0, 0], tails[0, 0], page_rows)
    columns = jnp.arange(model_width, dtype=jnp.int32)
    ordering_of = (columns[:, None] == proj_row[None, :]).astype(jnp.bfloat16)
    ordered = jnp.dot(mixed_in, ordering_of)
    own_mixed, other_mixed = ordered[:, : model_width // 2], ordered[:, model_width // 2 :]
    projected = jnp.dot(
        own_mixed, own_proj, preferred_element_type=jnp.float32
    ) + jnp.dot(
        other_mixed, other_proj, preferred_element_type=jnp.float32
    )
    resid = (balanced[:, 4 * model_width :].astype(jnp.float32) + projected).astype(jnp.bfloat16)
    resid_wide = resid.astype(jnp.float32)
    normed = (
        resid_wide * lax.rsqrt(jnp.mean(resid_wide * resid_wide, axis=1, keepdims=True) + 1e-06)
    ).astype(jnp.bfloat16)
    experts = router.shape[2]
    capacity = 4 * row_count // experts
    share = gate_share(normed, router[0], routes[0])
    slots = pair_slots(routes[0], capacity)
    slot_index = jnp.arange(experts * capacity, dtype=jnp.int32)
    packing = (
        (slots[None, :, 0] == slot_index[:, None]) | (slots[None, :, 1] == slot_index[:, None])
    ).astype(jnp.bfloat16)
    packed = jnp.dot(packing, normed)
    came_back = exchanged_experts(
        packed, w_gate[0], w_up[0], w_down[0], other_gate, other_up, other_down
    )
    mixture = jnp.zeros_like(resid_wide)
    for k in range(slots.shape[1]):
        picking = (slots[:, k : k + 1] == slot_index[None, :]).astype(jnp.bfloat16)
        picked = jnp.dot(picking, came_back, preferred_element_type=jnp.float32)
        mixture = mixture + picked * share[:, k : k + 1]
    output_rows = (resid_wide + mixture).astype(jnp.bfloat16)
    return from_behind(output_rows[None], "section", 1)


def solution(mesh):
    in_specs = (
        P("section", "expert", None),
        P("section", None, "expert"),
        P("section", "expert", None),
        P("section", "expert", None),
        P("section", "expert", None),
        P("section", "expert", None),
        P("section", None, None),
        P("section", None, "expert"),
        P("section", None, "expert"),
        P("section", "expert", None),
    )
    out_specs = P("section", "expert", None)
    return jax.shard_map(shards, mesh=mesh, in_specs=in_specs, out_specs=out_specs, check_vma=False)
```

```python
import functools

import jax
import jax.numpy as jnp
from jax import lax
from jax.experimental import pallas as pl
from jax.experimental.pallas import tpu as pltpu
from jax.sharding import PartitionSpec as P

HEADS = 8


def swapped(shard, axis, apart):
    return lax.ppermute(shard, axis, [(i, i ^ 1 << apart) for i in range(lax.axis_size(axis))])


def from_behind(block, axis, distance):
    devices = range(lax.axis_size(axis))
    route = [((i - distance) % len(devices), i) for i in devices]
    return lax.ppermute(block, axis, route)


def layout_rows(counts, tail_rows, page_rows, row_count):
    member_index = jnp.arange(counts.shape[0], dtype=jnp.int32)
    ahead = member_index[None, :] < member_index[:, None]
    starting = jnp.sum(jnp.where(ahead, counts[None, :], 0), axis=1)
    length = (counts - 1) * page_rows + tail_rows
    row_index = jnp.arange(row_count, dtype=jnp.int32)
    page_of = row_index // page_rows
    owner_of = jnp.sum((starting[None, :] <= page_of[:, None]).astype(jnp.int32), axis=1) - 1
    member = owner_of[:, None] == jnp.arange(counts.shape[0], dtype=jnp.int32)[None, :]
    offset = jnp.sum(jnp.where(member, starting[None, :] * page_rows, 0), axis=1)
    spread = jnp.sum(jnp.where(member, length[None, :], 0), axis=1)
    return (owner_of, row_index - offset, spread)


def attend(balanced, counts, tail_rows, page_rows):
    row_count = balanced.shape[0]
    model_width = balanced.shape[1] // 5
    head_dim = model_width // HEADS
    owner_of, position, spread = layout_rows(counts, tail_rows, page_rows, row_count)
    allowed = (
        (owner_of[:, None] == owner_of[None, :])
        & (position[None, :] <= position[:, None])
        & (position[None, :] < spread[None, :])
    )
    queries = balanced[:, :model_width].reshape(row_count, HEADS, head_dim)
    key_rows = balanced[:, model_width : 2 * model_width].reshape(row_count, HEADS, head_dim)
    values = balanced[:, 2 * model_width : 3 * model_width].reshape(row_count, HEADS, head_dim)
    scores = jnp.einsum(
        "qhd,khd->hqk", queries, key_rows, preferred_element_type=jnp.float32
    ) * head_dim ** (-0.5)
    weights = (
        jnp.where(allowed[None], jax.nn.silu(scores), 0.0)
        / spread.astype(jnp.float32)[None, :, None]
    )
    weights = weights.astype(jnp.bfloat16)
    attended = jnp.einsum(
        "hqk,khd->qhd", weights, values, preferred_element_type=jnp.float32
    ).reshape(row_count, model_width)
    average = jnp.mean(attended, axis=1, keepdims=True)
    centered = attended - average
    variance = jnp.mean(centered * centered, axis=1, keepdims=True)
    gating = balanced[:, 3 * model_width : 4 * model_width].astype(jnp.float32)
    return (centered * lax.rsqrt(variance + 1e-05) * gating).astype(jnp.bfloat16)


def gate_share(normed, router, routes):
    logits = jnp.dot(normed, router, preferred_element_type=jnp.float32)
    scores = jax.nn.sigmoid(logits)
    picked = routes[:, :, None] == jnp.arange(router.shape[1], dtype=jnp.int32)[None, None, :]
    chosen = jnp.sum(jnp.where(picked, scores[:, None, :], 0.0), axis=2)
    return chosen / jnp.sum(chosen, axis=1, keepdims=True)


def pair_slots(routes, capacity):
    chosen = routes.reshape(-1)
    order = jnp.arange(chosen.shape[0], dtype=jnp.int32)
    same = (chosen[:, None] == chosen[None, :]) & (order[None, :] < order[:, None])
    ranking = jnp.sum(same.astype(jnp.int32), axis=1)
    return (chosen * capacity + ranking).reshape(routes.shape)


def per_row(pages, page_rows):
    return jnp.broadcast_to(pages[:, None], (pages.shape[0], page_rows)).reshape(-1)


def expert_kernel(devices, packed_ref, *refs):
    stored, (back_ref, rows_ref, served_ref, hidden_ref), held = refs[:6], refs[6:10], refs[10:16]
    arrival, own_sem, send_sem, recv_sem = refs[16:]
    me = lax.axis_index("expert")
    loads = [
        pltpu.make_async_copy(there, here, arrival.at[i])
        for i, (there, here) in enumerate(zip(stored, held))
    ]
    for load in loads:
        load.start()

    group = devices // 2
    near = (me // group) * group
    far = group - near

    def each_peer(first, action):
        def step(k, carry):
            peer = first + lax.rem(me + k, group)

            @pl.when(peer != me)
            def _():
                action(peer)

            return carry

        lax.fori_loop(0, group, step, 0)

    def everyone(action):
        each_peer(far, action)
        each_peer(near, action)

    def transfer(source, target, hop, peer, sender):
        return pltpu.make_async_remote_copy(
            src_ref=source,
            dst_ref=target,
            send_sem=send_sem.at[hop, peer],
            recv_sem=recv_sem.at[hop, sender],
            device_id={"expert": peer},
            device_id_type=pl.DeviceIdType.MESH,
        )

    def out_to(peer):
        return transfer(packed_ref.at[peer], rows_ref.at[me], 0, peer, me)

    def back_to(peer):
        return transfer(served_ref.at[peer], back_ref.at[me], 1, peer, me)

    barrier = pltpu.get_barrier_semaphore()
    everyone(
        lambda peer: pl.semaphore_signal(
            barrier, inc=1, device_id={"expert": peer}, device_id_type=pl.DeviceIdType.MESH
        )
    )
    pl.semaphore_wait(barrier, devices - 1)
    everyone(lambda peer: out_to(peer).start())
    kept = pltpu.make_async_copy(packed_ref.at[me], rows_ref.at[me], own_sem.at[0])
    kept.start()
    kept.wait()
    units = stored[0].shape[1]
    width = packed_ref.shape[2]
    tile = 256 if units % 256 == 0 else units
    for turn in range(2):
        begin = near if turn == 0 else far
        each_peer(
            begin,
            lambda peer: transfer(packed_ref.at[peer], rows_ref.at[peer], 0, peer, peer).wait_recv(),
        )
        rows = rows_ref[pl.ds(begin, group)].reshape(-1, width)
        for half in range(2):
            gate_ref, up_ref, down_ref = held[3 * half : 3 * half + 3]
            if turn == 0:
                loads[3 * half].wait()
                loads[3 * half + 1].wait()
            for first in range(0, units, tile):
                span = slice(first, first + tile)
                gate_act = jnp.dot(rows, gate_ref[:, span], preferred_element_type=jnp.float32)
                up_act = jnp.dot(rows, up_ref[:, span], preferred_element_type=jnp.float32)
                hidden_ref[:, span] = (jax.nn.silu(gate_act) * up_act).astype(jnp.bfloat16)
            if turn == 0:
                loads[3 * half + 2].wait()
            for first in range(0, width, tile):
                span = slice(first, first + tile)
                part = jnp.dot(
                    hidden_ref[...], down_ref[:, span], preferred_element_type=jnp.float32
                ).astype(jnp.bfloat16)
                part = part.reshape(group, -1, tile)
                if half == 0:
                    served_ref[pl.ds(begin, group), :, span] = part
                else:
                    earlier = served_ref[pl.ds(begin, group), :, span].astype(jnp.float32)
                    served_ref[pl.ds(begin, group), :, span] = (
                        earlier + part.astype(jnp.float32)
                    ).astype(jnp.bfloat16)
        each_peer(begin, lambda peer: back_to(peer).start())
    kept = pltpu.make_async_copy(served_ref.at[me], back_ref.at[me], own_sem.at[1])
    kept.start()
    kept.wait()
    everyone(lambda peer: out_to(peer).wait_send())
    everyone(lambda peer: back_to(peer).wait_send())
    everyone(
        lambda peer: transfer(served_ref.at[peer], back_ref.at[peer], 1, peer, peer).wait_recv()
    )


def exchanged_experts(packed, *weights):
    devices = lax.axis_size("expert")
    width = packed.shape[1]
    blocks = packed.reshape(devices, -1, width)
    count = packed.shape[0]
    units = weights[0].shape[1]
    came_back = pl.pallas_call(
        functools.partial(expert_kernel, devices),
        out_shape=jax.ShapeDtypeStruct(blocks.shape, jnp.bfloat16),
        in_specs=[pl.BlockSpec(memory_space=pltpu.VMEM)]
        + [pl.BlockSpec(memory_space=pl.ANY)] * 6,
        out_specs=pl.BlockSpec(memory_space=pltpu.VMEM),
        scratch_shapes=[
            pltpu.VMEM(blocks.shape, jnp.bfloat16),
            pltpu.VMEM(blocks.shape, jnp.bfloat16),
            pltpu.VMEM((count // 2, units), jnp.bfloat16),
        ]
        + [pltpu.VMEM(weight.shape, weight.dtype) for weight in weights]
        + [
            pltpu.SemaphoreType.DMA((len(weights),)),
            pltpu.SemaphoreType.DMA((2,)),
            pltpu.SemaphoreType.DMA((2, devices)),
            pltpu.SemaphoreType.DMA((2, devices)),
        ],
        compiler_params=pltpu.CompilerParams(
            vmem_limit_bytes=54 * 1024 * 1024, collective_id=0, has_side_effects=True
        ),
        cost_estimate=pl.CostEstimate(
            flops=12 * count * width * units,
            bytes_accessed=12 * width * units + 4 * count * width,
            transcendentals=2 * count * units,
        ),
        name="expert_exchange",
    )(blocks, *weights)
    return came_back.reshape(count, width)


def gathered_projection(block):
    devices = lax.axis_size("expert")
    me = lax.axis_index("expert")
    rows = block.shape[0]
    line = [block] + [from_behind(block, "expert", 4 * k) for k in range(1, devices // 4)]
    line = jnp.concatenate(line, axis=0)
    plane = jnp.concatenate([line, swapped(line, "expert", 1)], axis=0)
    other = swapped(plane, "expert", 0)
    slot = jnp.arange(devices * rows, dtype=jnp.int32)
    turn, inner = slot // rows, slot % rows
    steps = turn % (devices // 4)
    side = (turn // (devices // 4)) % 2
    core = turn // (devices // 2)
    line_at = (me // 4 - steps + devices // 4) % (devices // 4)
    side_at = (me // 2 + side) % 2
    core_at = (me + core) % 2
    return plane, other, (line_at * 4 + side_at * 2 + core_at) * rows + inner


def shards(histories, page_map, user_pages, tails, routes, out_proj, router, w_gate, w_up, w_down):
    devices = lax.axis_size("expert")
    own_proj, other_proj, proj_row = gathered_projection(out_proj[0])
    other_gate = swapped(w_gate[0], "expert", 0)
    other_up = swapped(w_up[0], "expert", 0)
    other_down = swapped(w_down[0], "expert", 0)
    row_count = histories.shape[1]
    stacked_width = histories.shape[2]
    model_width = stacked_width // 5
    pages_dev = page_map.shape[2]
    page_rows = row_count // pages_dev
    page_slots = (pages_dev + devices - 1) // devices
    target = page_map[0, 0]
    target_dev = target // pages_dev
    earlier = (target_dev[None, :] == target_dev[:, None]) & (target[None, :] < target[:, None])
    position = target_dev * page_slots + jnp.sum(earlier.astype(jnp.int32), axis=1)
    sent_count = devices * page_slots * page_rows
    source_row = jnp.arange(row_count, dtype=jnp.int32)
    wire_row = jnp.arange(sent_count, dtype=jnp.int32)
    goes_to = per_row(position, page_rows) * page_rows + source_row % page_rows
    placing = (wire_row[:, None] == goes_to[None, :]).astype(jnp.bfloat16)
    outgoing = jnp.dot(placing, histories[0])
    arrived = lax.all_to_all(outgoing, "expert", split_axis=0, concat_axis=0, tiled=True)
    anchor = page_map[0, 1]
    anchor_dev = anchor // pages_dev
    ordering = jnp.arange(pages_dev, dtype=jnp.int32)
    sooner = (anchor_dev[None, :] == anchor_dev[:, None]) & (ordering[None, :] < ordering[:, None])
    where_from = anchor_dev * page_slots + jnp.sum(sooner.astype(jnp.int32), axis=1)
    comes_from = per_row(where_from, page_rows) * page_rows + source_row % page_rows
    taking = (comes_from[:, None] == wire_row[None, :]).astype(jnp.bfloat16)
    balanced = jnp.dot(taking, arrived)
    mixed_in = attend(balanced, user_pages[0, 0], tails[0, 0], page_rows)
    columns = jnp.arange(model_width, dtype=jnp.int32)
    ordering_of = (columns[:, None] == proj_row[None, :]).astype(jnp.bfloat16)
    ordered = jnp.dot(mixed_in, ordering_of)
    own_mixed, other_mixed = ordered[:, : model_width // 2], ordered[:, model_width // 2 :]
    projected = jnp.dot(
        own_mixed, own_proj, preferred_element_type=jnp.float32
    ) + jnp.dot(
        other_mixed, other_proj, preferred_element_type=jnp.float32
    )
    resid = (balanced[:, 4 * model_width :].astype(jnp.float32) + projected).astype(jnp.bfloat16)
    resid_wide = resid.astype(jnp.float32)
    normed = (
        resid_wide * lax.rsqrt(jnp.mean(resid_wide * resid_wide, axis=1, keepdims=True) + 1e-06)
    ).astype(jnp.bfloat16)
    experts = router.shape[2]
    capacity = 4 * row_count // experts
    share = gate_share(normed, router[0], routes[0])
    slots = pair_slots(routes[0], capacity)
    slot_index = jnp.arange(experts * capacity, dtype=jnp.int32)
    packing = (
        (slots[None, :, 0] == slot_index[:, None]) | (slots[None, :, 1] == slot_index[:, None])
    ).astype(jnp.bfloat16)
    packed = jnp.dot(packing, normed)
    came_back = exchanged_experts(
        packed, w_gate[0], w_up[0], w_down[0], other_gate, other_up, other_down
    )
    mixture = jnp.zeros_like(resid_wide)
    for k in range(slots.shape[1]):
        picking = (slots[:, k : k + 1] == slot_index[None, :]).astype(jnp.bfloat16)
        picked = jnp.dot(picking, came_back, preferred_element_type=jnp.float32)
        mixture = mixture + picked * share[:, k : k + 1]
    output_rows = (resid_wide + mixture).astype(jnp.bfloat16)
    return from_behind(output_rows[None], "section", 1)


def solution(mesh):
    in_specs = (
        P("section", "expert", None),
        P("section", None, "expert"),
        P("section", "expert", None),
        P("section", "expert", None),
        P("section", "expert", None),
        P("section", "expert", None),
        P("section", None, None),
        P("section", None, "expert"),
        P("section", None, "expert"),
        P("section", "expert", None),
    )
    out_specs = P("section", "expert", None)
    return jax.shard_map(shards, mesh=mesh, in_specs=in_specs, out_specs=out_specs, check_vma=False)
```
